512 devices in a mesh: row: 16 (over z), col: 32 (over x, y, core).
Axes of the slice: x: 4, y: 4, z: 16, core: 2. Of those that a mesh axis runs over, the one named last changes fastest.
Arguments:
- inverse_top: bfloat16 [4096, 4096], P('col', 'row'), may hold values from -0.09375 to 0.09375
- inverse_one: bfloat16 [6144, 3072], P('col', 'row'), may hold values from -0.109375 to 0.109375
- inverse_two: bfloat16 [8192, 2048], P('col', 'row'), may hold values from -0.125 to 0.125
- inverse_leaf: bfloat16 [8192, 1024], P('col', 'row'), may hold values from -0.1875 to 0.1875
- coupling_one: bfloat16 [3072, 6144], P('row', 'col'), may hold values from -0.109375 to 0.109375
- coupling_two: bfloat16 [2048, 8192], P('row', 'col'), may hold values from -0.125 to 0.125
- coupling_leaf: bfloat16 [1024, 8192], P('row', 'col'), may hold values from -0.1875 to 0.1875
- rhs_top: bfloat16 [4096, 256], P('row', 'col'), may hold values from -6 to 6
- rhs_one: bfloat16 [3072, 512], P('row', 'col'), may hold values from -6 to 6
- rhs_two: bfloat16 [2048, 1024], P('row', 'col'), may hold values from -6 to 6
- rhs_leaf: bfloat16 [1024, 2048], P('row', 'col'), may hold values from -6 to 6
- parent_map_one: int32 [2, 3072], replicated, may hold values from 0 to 4095, as said below
- parent_map_two: int32 [4, 2048], replicated, may hold values from 0 to 6143, as said below
- parent_map_leaf: int32 [8, 1024], replicated, may hold values from 0 to 4095, as said below
Outputs:
- solution_top: bfloat16 [4096, 256], P('row', 'col')
- solution_one: bfloat16 [3072, 512], P('row', 'col')
- solution_two: bfloat16 [2048, 1024], P('row', 'col')
- solution_leaf: bfloat16 [1024, 2048], P('row', 'col')
The draws below stay inside these ranges and needn't reach their ends.
Inputs may be any that keep to these rules, and one draw needn't show every extreme that they name: `parent_map_one`: row k lists distinct rows of the top front, one for each of the 3072 update rows of front k. Cut the update rows and the top separator each into 16 equal blocks: at most 24 rows of one block land in one block of the top front, a number that is reached in every row, and every block of the top front receives exactly 192 rows from each child. `parent_map_two`: row k lists distinct rows of the front k // 2 of the second level (its 3072 separator rows first, then its 3072 update rows), one for each of the 2048 update rows of front k. Cut the update rows into 16 equal blocks, and the parent's separator rows and its update rows each into 16 equal blocks, block j of the parent being the j-th separator block with the j-th update block: at most 16 rows of one block land in one parent block, reached in every row, and every parent block receives exactly 128 rows from each child. `parent_map_leaf`: as for parent_map_two, one level lower: 1024 update rows of front k into front k // 2 of the third level, at most 8 rows of one block into one parent block, reached in every row, and exactly 64 rows from each child into every parent block.
All inputs are finite; a program needn't handle non-finite values.
Results may differ from the reference program's by a relative error of at most 0.03.
Values may be sent and summed in bfloat16 or wider, within the bound.
No kernel may reach another device: no remote copies, remote signals or barrier semaphores. Data moves between devices by JAX's collectives and lax.ppermute only.
A program may use at most 64 MiB of HBM per device.

```python
import jax
import jax.numpy as jnp
from jax import lax

COLUMNS = 256
STRIPS = 16
SEP_TOP = 4096
SEP_ONE = 3072
SEP_TWO = 2048
SEP_LEAF = 1024


def level_map(key, fronts, upd_order, sep_parent, upd_parent):
    strips = STRIPS
    block_rows = upd_order // strips
    mean_load = upd_order // (strips * strips)
    block_len = (sep_parent + upd_parent) // strips
    sep_rows = sep_parent // strips
    upd_rows = max(upd_parent // strips, 1)

    def one_child(child_key):
        subkeys = jax.random.split(child_key, 4)
        pairing = jax.random.permutation(subkeys[0], strips)
        swings = jax.random.randint(subkeys[1], (strips // 2,), 0, mean_load + 1).astype(jnp.int32)
        swings = swings.at[0].set(mean_load)
        shifts = jnp.zeros((strips,), jnp.int32).at[pairing[0::2]].set(swings).at[pairing[1::2]].set(-swings)
        source = jnp.arange(strips, dtype=jnp.int32)[:, None]
        target = jnp.arange(strips, dtype=jnp.int32)[None, :]
        load_table = mean_load + shifts[(target - source) % strips]
        load_ends = jnp.cumsum(load_table, axis=1)
        local_at = jnp.arange(block_rows, dtype=jnp.int32)
        target_of = jnp.sum((load_ends[:, None, :] <= local_at[None, :, None]).astype(jnp.int32), axis=2)
        starts = load_ends - load_table
        slot_of = local_at[None, :] - jnp.take_along_axis(starts, target_of, axis=1)
        before = jnp.cumsum(load_table, axis=0) - load_table
        rank_of = jnp.take_along_axis(before, target_of, axis=1) + slot_of
        orders = jax.vmap(lambda subkey: jax.random.permutation(subkey, block_len))(jax.random.split(subkeys[2], strips))
        placed = orders[target_of, rank_of]
        values = jnp.where(placed < sep_rows, target_of * sep_rows + placed, sep_parent + target_of * upd_rows + placed - sep_rows)
        shuffles = jax.vmap(lambda subkey: jax.random.permutation(subkey, block_rows))(jax.random.split(subkeys[3], strips))
        result = jnp.zeros((strips, block_rows), jnp.int32).at[jnp.arange(strips)[:, None], shuffles].set(values.astype(jnp.int32))
        return result.reshape(upd_order).astype(jnp.int32)
    return jax.vmap(one_child)(jax.random.split(key, fronts))


def draw_parent_map_one(key, part):
    return level_map(jax.random.fold_in(key, 11), 2, SEP_ONE, SEP_TOP, 0)


def draw_parent_map_two(key, part):
    return level_map(jax.random.fold_in(key, 12), 4, SEP_TWO, SEP_ONE, SEP_ONE)


def draw_parent_map_leaf(key, part):
    return level_map(jax.random.fold_in(key, 13), 8, SEP_LEAF, SEP_TWO, SEP_TWO)


def block_scale(key, extent, cuts, low, largest):
    loudness, own = 1.0, jax.random.fold_in(key, 6)
    for position, parts in cuts:
        draws = jnp.exp(jax.random.uniform(jax.random.fold_in(own, position), (parts,), jnp.float32, low / len(cuts), largest / len(cuts)))
        loudness = loudness * jnp.repeat(draws, extent[position] // parts).reshape([-1 if axis == position else 1 for axis in range(len(extent))])
    return loudness


def gaussian(key, shape, scale, reach, cuts=(), kind=jnp.bfloat16):
    gain = block_scale(key, shape, cuts, -0.22, 0.18) if cuts else 1.0
    array = jax.random.normal(key, shape, jnp.float32) * scale * gain
    return jnp.minimum(jnp.maximum(array, -reach), reach).astype(kind)


def setup_inputs(seed: int = 0) -> dict:
    keys = jax.random.split(jax.random.key(seed), 15)
    return {
        "inverse_top": gaussian(keys[0], (SEP_TOP, SEP_TOP), SEP_TOP ** -0.5, 0.09375, ((0, 32), (1, 16))),
        "inverse_one": gaussian(keys[1], (2 * SEP_ONE, SEP_ONE), SEP_ONE ** -0.5, 0.109375, ((0, 32), (1, 16))),
        "inverse_two": gaussian(keys[2], (4 * SEP_TWO, SEP_TWO), SEP_TWO ** -0.5, 0.125, ((0, 32), (1, 16))),
        "inverse_leaf": gaussian(keys[3], (8 * SEP_LEAF, SEP_LEAF), SEP_LEAF ** -0.5, 0.1875, ((0, 32), (1, 16))),
        "coupling_one": gaussian(keys[4], (SEP_ONE, 2 * SEP_ONE), SEP_ONE ** -0.5, 0.109375, ((0, 16), (1, 32))),
        "coupling_two": gaussian(keys[5], (SEP_TWO, 4 * SEP_TWO), SEP_TWO ** -0.5, 0.125, ((0, 16), (1, 32))),
        "coupling_leaf": gaussian(keys[6], (SEP_LEAF, 8 * SEP_LEAF), SEP_LEAF ** -0.5, 0.1875, ((0, 16), (1, 32))),
        "rhs_top": gaussian(keys[7], (SEP_TOP, COLUMNS), 1.0, 6.0, ((0, 16), (1, 32))),
        "rhs_one": gaussian(keys[8], (SEP_ONE, 2 * COLUMNS), 1.0, 6.0, ((0, 16), (1, 32))),
        "rhs_two": gaussian(keys[9], (SEP_TWO, 4 * COLUMNS), 1.0, 6.0, ((0, 16), (1, 32))),
        "rhs_leaf": gaussian(keys[10], (SEP_LEAF, 8 * COLUMNS), 1.0, 6.0, ((0, 16), (1, 32))),
        "parent_map_one": draw_parent_map_one(jax.random.fold_in(keys[14], 71), 0),
        "parent_map_two": draw_parent_map_two(jax.random.fold_in(keys[14], 71), 0),
        "parent_map_leaf": draw_parent_map_leaf(jax.random.fold_in(keys[14], 71), 0),
    }


def pivot_product(inverse, vector):
    strip_width = inverse.shape[1] // STRIPS
    summed = jnp.zeros((inverse.shape[0], vector.shape[1]), jnp.float32)
    for strip_at in range(STRIPS):
        low_edge = strip_at * strip_width
        partial_value = jnp.dot(inverse[:, low_edge:low_edge + strip_width], vector[low_edge:low_edge + strip_width], preferred_element_type=jnp.float32)
        summed = summed + lax.optimization_barrier(partial_value.astype(jnp.bfloat16)).astype(jnp.float32)
    return summed


def coupling_back(coupling, gathered):
    strip_width = coupling.shape[0] // STRIPS
    summed = jnp.zeros((coupling.shape[1], gathered.shape[1]), jnp.float32)
    for strip_at in range(STRIPS):
        low_edge = strip_at * strip_width
        partial_value = jnp.dot(coupling[low_edge:low_edge + strip_width].T, gathered[low_edge:low_edge + strip_width], preferred_element_type=jnp.float32)
        summed = summed + lax.optimization_barrier(partial_value.astype(jnp.bfloat16)).astype(jnp.float32)
    return summed


def reference(inverse_top, inverse_one, inverse_two, inverse_leaf, coupling_one, coupling_two, coupling_leaf, rhs_top, rhs_one, rhs_two, rhs_leaf, parent_map_one, parent_map_two, parent_map_leaf):
    inverses = [inverse_top, inverse_one, inverse_two, inverse_leaf]
    couplings = [None, coupling_one, coupling_two, coupling_leaf]
    right_sides = [rhs_top, rhs_one, rhs_two, rhs_leaf]
    parent_maps = [None, parent_map_one, parent_map_two, parent_map_leaf]
    orders = [SEP_TOP, SEP_ONE, SEP_TWO, SEP_LEAF]
    pivots = [[None] * (2 ** tree_level) for tree_level in range(4)]
    updates = [[None] * (2 ** tree_level) for tree_level in range(4)]
    for tree_level in (3, 2, 1, 0):
        sep_order = orders[tree_level]
        for front_at in range(2 ** tree_level):
            right_side = right_sides[tree_level][:, front_at * COLUMNS:(front_at + 1) * COLUMNS]
            if tree_level == 3:
                separator = right_side
                update = jnp.zeros((sep_order, COLUMNS), jnp.bfloat16)
            else:
                length = sep_order + (sep_order if tree_level > 0 else 0)
                extended = jnp.zeros((length, COLUMNS), jnp.float32)
                for child_at in (2 * front_at, 2 * front_at + 1):
                    extended = extended.at[parent_maps[tree_level + 1][child_at]].add(updates[tree_level + 1][child_at].astype(jnp.float32))
                separator = (right_side.astype(jnp.float32) + extended[:sep_order]).astype(jnp.bfloat16)
                update = lax.optimization_barrier(extended[sep_order:].astype(jnp.bfloat16))
            inverse = inverses[tree_level][front_at * sep_order:(front_at + 1) * sep_order]
            pivot_out = pivot_product(inverse, separator).astype(jnp.bfloat16)
            pivots[tree_level][front_at] = pivot_out
            if tree_level > 0:
                coupling = couplings[tree_level][:, front_at * sep_order:(front_at + 1) * sep_order]
                coupled = jnp.dot(coupling, pivot_out, preferred_element_type=jnp.float32)
                updates[tree_level][front_at] = (update.astype(jnp.float32) - coupled).astype(jnp.bfloat16)
    solutions = [[None] * (2 ** tree_level) for tree_level in range(4)]
    gathered_rows = [[None] * (2 ** tree_level) for tree_level in range(4)]
    for tree_level in range(4):
        sep_order = orders[tree_level]
        for front_at in range(2 ** tree_level):
            pivot_out = pivots[tree_level][front_at]
            if tree_level == 0:
                residual = pivot_out
            else:
                parent_at = front_at // 2
                pieces = [solutions[tree_level - 1][parent_at]]
                if tree_level > 1:
                    pieces.append(gathered_rows[tree_level - 1][parent_at])
                parent_rows = jnp.concatenate(pieces, axis=0)
                gathered = parent_rows[parent_maps[tree_level][front_at]]
                gathered_rows[tree_level][front_at] = gathered
                coupling = couplings[tree_level][:, front_at * sep_order:(front_at + 1) * sep_order]
                residual = (pivot_out.astype(jnp.float32) - coupling_back(coupling, gathered)).astype(jnp.bfloat16)
            inverse = inverses[tree_level][front_at * sep_order:(front_at + 1) * sep_order]
            solutions[tree_level][front_at] = jnp.dot(inverse.T, residual, preferred_element_type=jnp.float32).astype(jnp.bfloat16)
    outputs = [jnp.concatenate(solutions[tree_level], axis=1) for tree_level in range(4)]
    return (outputs[0], outputs[1], outputs[2], outputs[3])
```

```python
import jax
import jax.numpy as jnp
from jax import lax
from jax.sharding import PartitionSpec as P

BF16 = jnp.bfloat16
F32 = jnp.float32
LANES = 128


def core_swapped(value):
    return lax.ppermute(value, "col", [(source, source ^ 1) for source in range(32)])


def chip_groups(bits):
    chips = 1 << bits
    return [
        [2 * (base + chip) + core for chip in range(chips)]
        for base in range(0, 16, chips)
        for core in range(2)
    ]


def summed_over_chips(value, bits):
    chips = 1 << bits
    copies = jnp.broadcast_to(value.astype(BF16)[None], (chips, *value.shape))
    got = lax.all_to_all(
        copies, "col", split_axis=0, concat_axis=0, tiled=True, axis_index_groups=chip_groups(bits)
    )
    return jnp.sum(got.astype(F32), axis=0)


def halves(block, core):
    half = block.shape[0] // 2
    first, second = block[:half], block[half:]
    return jnp.where(core == 0, first, second), jnp.where(core == 0, second, first)


def side_by_side(mine, other, core):
    return jnp.where(
        core == 0,
        jnp.concatenate([mine, other], axis=-1),
        jnp.concatenate([other, mine], axis=-1),
    )


def to_strips(block):
    return [block[:, at : at + LANES] for at in range(0, block.shape[1], LANES)]


def dot(left, right):
    return lax.dot_general(left, right, (((1,), (0,)), ((), ())), preferred_element_type=F32)


def dot_t(left, right):
    return lax.dot_general(left, right, (((1,), (1,)), ((), ())), preferred_element_type=F32)


def composite_targets(maps, fronts, orders, core):
    tables = [None] * 4
    for level in (1, 2, 3):
        parent = orders[level - 1]
        own = lax.dynamic_index_in_dim(maps[level], fronts[level], 0, keepdims=False)
        block = parent // 16
        half = block // 2
        at = jnp.minimum(own, parent - 1)
        inside = at % block
        place = jnp.where(inside // half == core, at // block * half + inside % half, -1)
        if level > 1:
            above = tables[level - 1]
            further = above[jnp.clip(own - parent, 0, parent - 1)]
            further = jnp.where(further >= 0, further + parent // 2, -1)
            place = jnp.where(own < parent, place, further)
        tables[level] = place
    return tables


def per_device(
    inverse_top,
    inverse_one,
    inverse_two,
    inverse_leaf,
    coupling_one,
    coupling_two,
    coupling_leaf,
    rhs_top,
    rhs_one,
    rhs_two,
    rhs_leaf,
    parent_map_one,
    parent_map_two,
    parent_map_leaf,
):
    row = lax.axis_index("row")
    column = lax.axis_index("col")
    core = column % 2
    inverses = [inverse_top, inverse_one, inverse_two, inverse_leaf]
    couplings = [None, coupling_one, coupling_two, coupling_leaf]
    right_sides = [rhs_top, rhs_one, rhs_two, rhs_leaf]
    maps = [None, parent_map_one, parent_map_two, parent_map_leaf]
    groups = [32, 16, 8, 4]
    orders = [inverse.shape[1] * 16 for inverse in inverses]
    fronts = [column // group for group in groups]
    chip_bits = [4, 3, 2, 1]

    blocks = [inverse.T for inverse in inverses] + couplings[1:]
    kept, sent = zip(*[halves(block, core) for block in blocks])
    rhs_kept, rhs_sent = zip(*[halves(block, core) for block in right_sides])
    got = core_swapped(list(sent) + list(rhs_sent))
    paired = [side_by_side(mine, other, core) for mine, other in zip(kept, got[:7])]
    rhs_paired = [side_by_side(mine, other, core) for mine, other in zip(rhs_kept, got[7:])]

    strips = [to_strips(block) for block in paired]
    packed = jnp.concatenate([piece for pieces in strips for piece in pieces], axis=0)
    gathered = lax.all_gather(packed, "row", axis=0)
    whole, at = [], 0
    for pieces in strips:
        depth = pieces[0].shape[0]
        parts = []
        for _ in pieces:
            parts.append(gathered[:, at : at + depth].reshape(16 * depth, LANES))
            at += depth
        whole.append(jnp.concatenate(parts, axis=1))
    solve = whole[:4]

    outgoing = []
    for level in range(4):
        block = rhs_paired[level]
        planes = block.shape[1] // 16
        spread = block.T.reshape(planes, 16, block.shape[0])
        chip = column % groups[level] // 2
        outgoing.append(
            lax.dynamic_update_slice(
                jnp.zeros((16, 16, block.shape[0]), BF16), spread, (chip * planes, 0, 0)
            )
        )
    incoming = lax.all_to_all(
        jnp.concatenate(outgoing, axis=2), "row", split_axis=0, concat_axis=0, tiled=True
    )
    total, at = [], 0
    for level in range(4):
        depth = rhs_paired[level].shape[0]
        part = incoming[:, :, at : at + depth].transpose(1, 0, 2)
        total.append(part.reshape(16, 16 * depth).astype(F32))
        at += depth

    targets = composite_targets(maps, fronts, orders, core)
    placed = [None]
    for level in (1, 2, 3):
        mine = whole[3 + level]
        other = core_swapped(mine)
        height = orders[level] // 2
        block = orders[level] // 16
        cut = targets[level].reshape(16, 2, block // 2)
        here = jnp.where(core == 0, cut[:, 0], cut[:, 1]).reshape(height)
        there = jnp.where(core == 0, cut[:, 1], cut[:, 0]).reshape(height)
        rows = sum(orders[:level]) // 2
        hot = lax.broadcasted_iota(jnp.int32, (rows, 2 * height), 0) == jnp.concatenate([here, there])[None]
        both = jnp.concatenate([mine, other], axis=0)
        placed.append(dot(hot.astype(BF16), both).astype(BF16))

    solved = [None] * 4
    for level in (3, 2, 1, 0):
        separator = summed_over_chips(total[level], chip_bits[level]).astype(BF16)
        partial = dot(separator, solve[level])
        solved[level] = partial + core_swapped(partial)
        if level > 0:
            contribution = dot_t(solved[level].astype(BF16), placed[level])
            at = 0
            for above in range(level - 1, -1, -1):
                height = orders[above] // 2
                total[above] = total[above] - contribution[:, at : at + height]
                at += height

    solutions = [None] * 4
    above = None
    for level in range(4):
        residual = solved[level].astype(BF16)
        if level > 0:
            partial = dot(above, placed[level])
            residual = (residual.astype(F32) - (partial + core_swapped(partial))).astype(BF16)
        product = dot_t(residual, solve[level])
        solutions[level] = summed_over_chips(product, chip_bits[level]).astype(BF16)
        above = solutions[0] if level == 0 else jnp.concatenate([solutions[level], above], axis=1)

    sending = [value.reshape(16, 16, -1).transpose(1, 0, 2) for value in solutions]
    returned = lax.all_to_all(
        jnp.concatenate(sending, axis=2), "row", split_axis=0, concat_axis=0, tiled=True
    )
    kept, sent, at = [], [], 0
    for level in range(4):
        depth = sending[level].shape[2]
        planes = 32 // groups[level]
        chip = column % groups[level] // 2
        part = lax.dynamic_slice(
            returned[:, :, at : at + depth], (chip * planes, 0, 0), (planes, 16, depth)
        )
        mine, other = halves(part.reshape(planes * 16, depth), core)
        kept.append(mine)
        sent.append(other)
        at += depth
    got = core_swapped(sent)
    results = [side_by_side(mine, other, core).T for mine, other in zip(kept, got)]
    return tuple(results)


def solution(mesh):
    split = P("row", "col")
    in_specs = (P("col", "row"),) * 4 + (split,) * 7 + (P(),) * 3
    return jax.shard_map(
        per_device, mesh=mesh, in_specs=in_specs, out_specs=(split,) * 4, check_vma=False
    )
```

```python
import jax
import jax.numpy as jnp
from jax import lax
from jax.experimental.layout import Layout, with_layout_constraint
from jax.sharding import PartitionSpec as P

BF16 = jnp.bfloat16
F32 = jnp.float32
LANES = 128


def core_swapped(value):
    return lax.ppermute(value, "col", [(source, source ^ 1) for source in range(32)])


def all_to_all(value, axis, groups=None):
    return lax.all_to_all(
        value, axis, split_axis=0, concat_axis=0, tiled=True, axis_index_groups=groups
    )


def chip_groups(bits, stride=1):
    chips = 1 << bits
    return [
        [2 * (base + low + stride * chip) + core for chip in range(chips)]
        for base in range(0, 16, chips * stride)
        for low in range(stride)
        for core in range(2)
    ]


def summed_over_chips(value, bits):
    for part, stride in ((2, 1), (2, 4)) if bits == 4 else ((bits, 1),):
        chips = 1 << part
        copies = jnp.broadcast_to(value.astype(BF16)[None], (chips, *value.shape))
        got = all_to_all(copies, "col", chip_groups(part, stride))
        value = jnp.sum(got.astype(F32), axis=0)
    return value


def after(value, earlier):
    return lax.optimization_barrier((value, earlier))[0]


def halves(block, core, axis=0):
    half = block.shape[axis] // 2
    return (
        lax.dynamic_slice_in_dim(block, core * half, half, axis),
        lax.dynamic_slice_in_dim(block, (1 - core) * half, half, axis),
    )


def dot(left, right):
    return lax.dot_general(left, right, (((1,), (0,)), ((), ())), preferred_element_type=F32)


def dot_t(left, right):
    return lax.dot_general(left, right, (((1,), (1,)), ((), ())), preferred_element_type=F32)


def core_summed(value):
    other = core_swapped(value)
    width = value.shape[1] // 2
    return value + jnp.concatenate([other[:, width:], other[:, :width]], axis=1)


def core_summed_one(value):
    other = core_swapped(value)
    return value + jnp.concatenate(
        [other[:, 256:], other[:, 192:256], other[:, 128:192], other[:, :128]], axis=1
    )


def composite_targets(maps, fronts, orders, core):
    tables = [None] * 4
    for level in (1, 2, 3):
        parent = orders[level - 1]
        own = lax.dynamic_index_in_dim(maps[level - 1], fronts[level], 0, keepdims=False)
        block = parent // 16
        half = block // 2
        at = jnp.minimum(own, parent - 1)
        inside = at % block
        place = jnp.where(inside // half == core, at // block * half + inside % half, -1)
        if level > 1:
            above = tables[level - 1]
            further = above[jnp.clip(own - parent, 0, parent - 1)]
            further = jnp.where(further >= 0, further + parent // 2, -1)
            place = jnp.where(own < parent, place, further)
        tables[level] = place
    return tables


def is_at(target, rows, first, axis):
    shape = (rows, target.shape[0]) if axis == 0 else (target.shape[0], rows)
    spot = lax.broadcasted_iota(jnp.int32, shape, axis) + first
    return (spot == (target[None] if axis == 0 else target[:, None])).astype(BF16)


def per_device(
    inverse_top,
    inverse_one,
    inverse_two,
    inverse_leaf,
    coupling_one,
    coupling_two,
    coupling_leaf,
    rhs_top,
    rhs_one,
    rhs_two,
    rhs_leaf,
    parent_map_one,
    parent_map_two,
    parent_map_leaf,
):
    column = lax.axis_index("col")
    core = column % 2
    groups = [32, 16, 8, 4]
    orders = [4096, 3072, 2048, 1024]
    maps = [None, parent_map_one, parent_map_two, parent_map_leaf]
    fronts = [column // group for group in groups]
    chips = [column % group // 2 for group in groups]
    leaf_groups = [[4 * front + at for at in range(4)] for front in range(8)]
    join = lambda parts: jnp.concatenate(parts, axis=1)
    stack = lambda parts: jnp.concatenate(parts, axis=0)
    lanes = lambda block: [block[:, :LANES], block[:, LANES:]]

    spread = all_to_all(jnp.broadcast_to(rhs_leaf[None], (4, 64, 64)), "col", leaf_groups)

    def strips(one, two, top, leaf, coupled):
        tails = join([one[:, LANES:], coupled[:, LANES:]])
        parts = [one[:, :LANES]] + lanes(two) + [top] + lanes(leaf)
        return stack(parts + [coupled[:, :LANES], tails])

    by_rows = lambda value: with_layout_constraint(value, Layout(major_to_minor=(0, 1)))
    blocks = [inverse_one.T, inverse_two.T, inverse_top.T, inverse_leaf.T, coupling_one]
    kept, sent = zip(*[halves(block, core) for block in blocks])
    taken = core_swapped(by_rows(strips(*sent)))
    packed = stack([strips(*kept)] + lanes(coupling_two) + [taken])
    upper = lax.all_gather(by_rows(packed), "row", axis=0)

    leaf_columns = spread.transpose(0, 2, 1).reshape(256, 64)
    leaf_products = dot_t(leaf_columns, inverse_leaf).astype(BF16)

    sides = [side.T for side in (rhs_top, rhs_one, rhs_two)]
    side_kept, side_sent = zip(*[halves(side, core, 1) for side in sides])
    pad = lambda part: jnp.pad(part, ((0, 0), (0, LANES - part.shape[1])))
    side_taken = core_swapped(stack([pad(part) for part in side_sent]))
    outgoing, at = [leaf_products.reshape(16, 16, 256)], 0
    for level in range(3):
        mine = side_kept[level]
        count, depth = mine.shape
        other = side_taken[at : at + count, :depth]
        at += count
        both = jnp.where(core == 0, stack([mine, other]), stack([other, mine]))
        planes = 2 * count // 16
        outgoing.append(
            lax.dynamic_update_slice(
                jnp.zeros((16, 16, depth), BF16),
                both.reshape(planes, 16, depth),
                (chips[level] * planes, 0, 0),
            )
        )
    sending = jnp.concatenate(outgoing, axis=2)
    incoming = all_to_all(sending, "row")
    leaf_own = jnp.sum(incoming[:, :, :256].astype(F32), axis=0).astype(BF16)
    total, at = [], 256
    for level in range(3):
        depth = side_kept[level].shape[1]
        part = incoming[:, :, at : at + depth].transpose(1, 0, 2)
        total.append(part.reshape(16, 16 * depth).astype(F32))
        at += depth

    leaf_rows = lax.all_gather(after(coupling_leaf, sending), "row", axis=0, tiled=True)
    update = dot_t(leaf_own, leaf_rows)
    update = (update + core_swapped(update)).astype(BF16)

    targets = composite_targets(after(maps[1:], sending), fronts, orders, core)
    height = [order // 2 for order in orders]
    base = lambda level, above: sum(height[above + 1 : level])

    def leaf_share(above):
        return dot(update, is_at(targets[3], height[above], base(3, above), 1))

    separator = summed_over_chips(total[2] - leaf_share(2), 2).astype(BF16)
    total[1] = total[1] - leaf_share(1)
    total[0] = total[0] - leaf_share(0)

    solve, solved, placed = [None] * 4, [None] * 4, {}
    rows_of = lambda value, at, depth: value[:, at : at + depth].reshape(16 * depth, LANES)

    def share(update, level, above, target):
        return dot(update, is_at(target, height[above], base(level, above), 1))

    def place(level, above, coupling, target):
        hot = is_at(target, height[above], base(level, above), 0)
        placed[level, above] = lax.optimization_barrier(dot(hot, coupling).astype(BF16))

    far = 608 + 256
    solve[2] = join([rows_of(upper, at, 64) for at in (96, 160, far + 96, far + 160)])
    two_rows = join([rows_of(upper, 608, 128), rows_of(upper, 736, 128)])
    two_coupling = join([two_rows, core_swapped(two_rows)])
    solved[2] = core_summed(dot(separator, solve[2]))
    update_two = dot_t(solved[2].astype(BF16), two_coupling).astype(BF16)
    part = total[1] - share(update_two, 2, 1, targets[2])
    separator = summed_over_chips(part, 3).astype(BF16)

    late, late_two = after((upper, targets[2]), part)
    main, tail, far_tail = rows_of(late, 416, 96), rows_of(late, 512, 96), rows_of(late, far + 512, 96)
    solve[1] = join([rows_of(late, 0, 96), tail, far_tail, rows_of(late, far, 96)])
    coupling = join([main, tail, far_tail, rows_of(late, far + 416, 96)])
    swapped = core_swapped(coupling)
    other = join([swapped[:, at : at + LANES] for at in (384, 256, 128, 0)])
    one_coupling = stack([coupling, other])
    cut = targets[1].reshape(16, 2, 96)
    here = jnp.where(core == 0, cut[:, 0], cut[:, 1]).reshape(1536)
    there = jnp.where(core == 0, cut[:, 1], cut[:, 0]).reshape(1536)
    late_one = after(stack([here, there]), part)
    total[0] = total[0] - share(update_two, 2, 0, late_two)
    place(1, 0, one_coupling, late_one)
    gap = jnp.zeros((16, 64), BF16)
    solve_wide = lambda y: join([y[:, :192], gap, y[:, 192:256], gap, y[:, 256:]])
    couple_wide = lambda y: join([y[:, :128], gap, y[:, 128:192], gap, y[:, 192:]])
    solve_narrow = lambda y: join([y[:, :192], y[:, 256:320], y[:, 384:]])
    couple_narrow = lambda y: join([y[:, :128], y[:, 192:256], y[:, 320:]])
    solved[1] = core_summed_one(solve_narrow(dot(separator, solve[1])))
    part = total[0] - dot_t(couple_wide(solved[1].astype(BF16)), placed[1, 0])
    separator = summed_over_chips(part, 4).astype(BF16)

    late, late_two = after((upper, targets[2]), part)
    solve[0] = join([rows_of(late, 224, 128), rows_of(late, far + 224, 128)])
    place(2, 0, two_coupling, late_two)
    place(2, 1, two_coupling, late_two)
    solved[0] = core_summed(dot(separator, solve[0]))
    solve[3] = join([rows_of(late, at, 32) for at in (352, 384, far + 352, far + 384)])
    leaf_coupling = join([leaf_rows, core_swapped(after(leaf_rows, update))])
    solved[3] = join([leaf_own, core_swapped(after(leaf_own, update))])

    solutions = []
    for level in range(4):
        residual = solved[level].astype(BF16)
        if level == 1:
            partial = core_summed_one(couple_narrow(dot(solutions[0], placed[1, 0])))
            residual = (residual.astype(F32) - partial).astype(BF16)
            residual = solve_wide(residual)
        if level == 2:
            partial = core_summed(
                dot(solutions[0], placed[2, 0]) + dot(solutions[1], placed[2, 1])
            )
            residual = (residual.astype(F32) - partial).astype(BF16)
        if level == 3:
            taken = sum(
                dot(solutions[above], is_at(targets[3], height[above], base(3, above), 0))
                for above in range(3)
            )
            partial = core_summed(dot(taken.astype(BF16), leaf_coupling))
            residual = (residual.astype(F32) - partial).astype(BF16)
        product = dot_t(residual, solve[level])
        if level < 3:
            product = summed_over_chips(product, 4 - level)
        solutions.append(product.astype(BF16))

    sending = [value.reshape(16, 16, -1).transpose(1, 0, 2) for value in solutions]
    returned = all_to_all(jnp.concatenate(sending, axis=2), "row")
    parts, at = [], 0
    for level in range(4):
        depth = sending[level].shape[2]
        part = returned[:, :, at : at + depth]
        at += depth
        if level < 3:
            planes = 32 // groups[level]
            part = lax.dynamic_slice_in_dim(part, chips[level] * planes, planes, 0)
            part = part.reshape(1, 2, planes * 8, depth)
            part = jnp.broadcast_to(part, (2, *part.shape[1:])).reshape(4, planes * 8, depth)
        else:
            part = part.reshape(4, 64, depth)
        parts.append(jnp.pad(part, ((0, 0), (0, 0), (0, LANES - depth))))
    shared = all_to_all(jnp.concatenate(parts, axis=1), "col", leaf_groups)
    near = lax.dynamic_slice_in_dim(shared, chips[3] * 2, 2, 0)
    results, at = [], 0
    for level in range(4):
        count, depth = parts[level].shape[1], sending[level].shape[2]
        if level < 3:
            part = near[:, at : at + count, :depth]
        else:
            both = shared[:, at : at + count, :depth].astype(F32).reshape(2, 2, count, depth)
            part = (both[0] + both[1]).astype(BF16)
        at += count
        results.append(jnp.concatenate([part[0], part[1]], axis=1).T)
    return tuple(results)


def solution(mesh):
    split = P("row", "col")
    in_specs = (P("col", "row"),) * 4 + (split,) * 7 + (P(),) * 3
    return jax.shard_map(
        per_device, mesh=mesh, in_specs=in_specs, out_specs=(split,) * 4, check_vma=False
    )
```

```python
import jax
import jax.numpy as jnp
from jax import lax
from jax.experimental.layout import Layout, with_layout_constraint
from jax.sharding import PartitionSpec as P

BF16 = jnp.bfloat16
F32 = jnp.float32
LANES = 128


def core_swapped(value):
    return lax.ppermute(value, "col", [(source, source ^ 1) for source in range(32)])


def all_to_all(value, axis, groups=None):
    return lax.all_to_all(
        value, axis, split_axis=0, concat_axis=0, tiled=True, axis_index_groups=groups
    )


def chip_groups(bits, stride=1):
    chips = 1 << bits
    return [
        [2 * (base + low + stride * chip) + core for chip in range(chips)]
        for base in range(0, 16, chips * stride)
        for low in range(stride)
        for core in range(2)
    ]


def summed_over_chips(value, bits):
    for part, stride in ((2, 1), (2, 4)) if bits == 4 else ((bits, 1),):
        chips = 1 << part
        copies = jnp.broadcast_to(value.astype(BF16)[None], (chips, *value.shape))
        got = all_to_all(copies, "col", chip_groups(part, stride))
        value = jnp.sum(got.astype(F32), axis=0)
    return value


def after(value, earlier):
    return lax.optimization_barrier((value, earlier))[0]


def halves(block, core, axis=0):
    half = block.shape[axis] // 2
    return (
        lax.dynamic_slice_in_dim(block, core * half, half, axis),
        lax.dynamic_slice_in_dim(block, (1 - core) * half, half, axis),
    )


def dot(left, right):
    return lax.dot_general(left, right, (((1,), (0,)), ((), ())), preferred_element_type=F32)


def dot_t(left, right):
    return lax.dot_general(left, right, (((1,), (1,)), ((), ())), preferred_element_type=F32)


def core_summed(value):
    other = core_swapped(value)
    width = value.shape[1] // 2
    return value + jnp.concatenate([other[:, width:], other[:, :width]], axis=1)


def core_summed_one(value):
    other = core_swapped(value)
    return value + jnp.concatenate(
        [other[:, 256:], other[:, 192:256], other[:, 128:192], other[:, :128]], axis=1
    )


def is_at(target, rows, first, axis):
    shape = (rows, target.shape[0]) if axis == 0 else (target.shape[0], rows)
    spot = lax.broadcasted_iota(jnp.int32, shape, axis) + first
    return (spot == (target[None] if axis == 0 else target[:, None])).astype(BF16)


def looked_up(table, at):
    digits = jnp.stack([(table + 1) // 128, (table + 1) % 128]).astype(BF16)
    found = dot(digits, is_at(at, table.shape[0], 0, 0))
    return (found[0] * 128 + found[1]).astype(jnp.int32) - 1


def composite_targets(maps, fronts, orders, core):
    tables = [None] * 4
    for level in (1, 2, 3):
        parent = orders[level - 1]
        own = lax.dynamic_index_in_dim(maps[level - 1], fronts[level], 0, keepdims=False)
        block = parent // 16
        half = block // 2
        at = jnp.minimum(own, parent - 1)
        inside = at % block
        place = jnp.where(inside // half == core, at // block * half + inside % half, -1)
        if level > 1:
            further = looked_up(tables[level - 1], own - parent)
            further = jnp.where(further >= 0, further + parent // 2, -1)
            place = jnp.where(own < parent, place, further)
        tables[level] = place
    return tables


def per_device(
    inverse_top,
    inverse_one,
    inverse_two,
    inverse_leaf,
    coupling_one,
    coupling_two,
    coupling_leaf,
    rhs_top,
    rhs_one,
    rhs_two,
    rhs_leaf,
    parent_map_one,
    parent_map_two,
    parent_map_leaf,
):
    column = lax.axis_index("col")
    core = column % 2
    groups = [32, 16, 8, 4]
    orders = [4096, 3072, 2048, 1024]
    maps = [None, parent_map_one, parent_map_two, parent_map_leaf]
    fronts = [column // group for group in groups]
    chips = [column % group // 2 for group in groups]
    leaf_groups = [[4 * front + at for at in range(4)] for front in range(8)]
    join = lambda parts: jnp.concatenate(parts, axis=1)
    stack = lambda parts: jnp.concatenate(parts, axis=0)
    lanes = lambda block: [block[:, :LANES], block[:, LANES:]]

    spread = all_to_all(jnp.broadcast_to(rhs_leaf[None], (4, 64, 64)), "col", leaf_groups)

    def strips(one, two, top, leaf, coupled):
        tails = join([one[:, LANES:], coupled[:, LANES:]])
        parts = [one[:, :LANES]] + lanes(two) + [top] + lanes(leaf)
        return stack(parts + [coupled[:, :LANES], tails])

    by_rows = lambda value: with_layout_constraint(value, Layout(major_to_minor=(0, 1)))
    blocks = [inverse_one.T, inverse_two.T, inverse_top.T, inverse_leaf.T, coupling_one]
    kept, sent = zip(*[halves(block, core) for block in blocks])
    taken = core_swapped(by_rows(strips(*sent)))
    packed = stack([strips(*kept)] + lanes(coupling_two) + [taken])
    upper = lax.all_gather(by_rows(packed), "row", axis=0)

    leaf_columns = spread.transpose(0, 2, 1).reshape(256, 64)
    leaf_products = dot_t(leaf_columns, inverse_leaf).astype(BF16)

    sides = [side.T for side in (rhs_top, rhs_one, rhs_two)]
    side_kept, side_sent = zip(*[halves(side, core, 1) for side in sides])
    pad = lambda part: jnp.pad(part, ((0, 0), (0, LANES - part.shape[1])))
    side_taken = core_swapped(stack([pad(part) for part in side_sent]))
    outgoing, at = [leaf_products.reshape(16, 16, 256)], 0
    for level in range(3):
        mine = side_kept[level]
        count, depth = mine.shape
        other = side_taken[at : at + count, :depth]
        at += count
        both = jnp.where(core == 0, stack([mine, other]), stack([other, mine]))
        planes = 2 * count // 16
        outgoing.append(
            lax.dynamic_update_slice(
                jnp.zeros((16, 16, depth), BF16),
                both.reshape(planes, 16, depth),
                (chips[level] * planes, 0, 0),
            )
        )
    sending = jnp.concatenate(outgoing, axis=2)
    incoming = all_to_all(sending, "row")
    leaf_own = jnp.sum(incoming[:, :, :256].astype(F32), axis=0).astype(BF16)
    total, at = [], 256
    for level in range(3):
        depth = side_kept[level].shape[1]
        part = incoming[:, :, at : at + depth].transpose(1, 0, 2)
        total.append(part.reshape(16, 16 * depth).astype(F32))
        at += depth

    leaf_rows = lax.all_gather(after(coupling_leaf, sending), "row", axis=0, tiled=True)
    update = dot_t(leaf_own, leaf_rows)
    update = (update + core_swapped(update)).astype(BF16)

    targets = composite_targets(after(maps[1:], sending), fronts, orders, core)
    height = [order // 2 for order in orders]
    base = lambda level, above: sum(height[above + 1 : level])

    def leaf_share(above):
        return dot(update, is_at(targets[3], height[above], base(3, above), 1))

    separator = summed_over_chips(total[2] - leaf_share(2), 2).astype(BF16)
    total[1] = total[1] - leaf_share(1)
    total[0] = total[0] - leaf_share(0)

    leaf_coupling = join([leaf_rows, core_swapped(after(leaf_rows, update))])
    leaf_solved = join([leaf_own, core_swapped(after(leaf_own, update))])
    separator, leaf_coupling, leaf_solved = lax.optimization_barrier(
        (separator, leaf_coupling, leaf_solved)
    )

    solve, solved = [None] * 4, [None, None, None, leaf_solved]
    rows_of = lambda value, at, depth: value[:, at : at + depth].reshape(16 * depth, LANES)

    def share(update, level, above, target):
        return dot(update, is_at(target, height[above], base(level, above), 1))

    far = 608 + 256
    solve[2] = join([rows_of(upper, at, 64) for at in (96, 160, far + 96, far + 160)])
    two_rows = join([rows_of(upper, 608, 128), rows_of(upper, 736, 128)])
    two_coupling = join([two_rows, core_swapped(two_rows)])
    solved[2] = core_summed(dot(separator, solve[2]))
    update_two = dot_t(solved[2].astype(BF16), two_coupling).astype(BF16)
    part = total[1] - share(update_two, 2, 1, targets[2])
    separator = summed_over_chips(part, 3).astype(BF16)

    late, late_two = after((upper, targets[2]), part)
    main, tail, far_tail = rows_of(late, 416, 96), rows_of(late, 512, 96), rows_of(late, far + 512, 96)
    solve[1] = join([rows_of(late, 0, 96), tail, far_tail, rows_of(late, far, 96)])
    coupling = join([main, tail, far_tail, rows_of(late, far + 416, 96)])
    swapped = core_swapped(coupling)
    other = join([swapped[:, at : at + LANES] for at in (384, 256, 128, 0)])
    cut = targets[1].reshape(16, 2, 96)
    here = jnp.where(core == 0, cut[:, 0], cut[:, 1]).reshape(1536)
    there = jnp.where(core == 0, cut[:, 1], cut[:, 0]).reshape(1536)
    here, there = after((here, there), part)
    total[0] = total[0] - share(update_two, 2, 0, late_two)
    placed = dot(is_at(here, height[0], 0, 0), coupling).astype(BF16)
    solve[0] = join([rows_of(late, 224, 128), rows_of(late, far + 224, 128)])
    solve[3] = join([rows_of(late, at, 32) for at in (352, 384, far + 352, far + 384)])
    separator, total[0], placed, solve[0], solve[3] = lax.optimization_barrier(
        (separator, total[0], placed, solve[0], solve[3])
    )
    placed = (placed.astype(F32) + dot(is_at(there, height[0], 0, 0), other)).astype(BF16)
    placed = lax.optimization_barrier(placed)
    gap = jnp.zeros((16, 64), BF16)
    solve_wide = lambda y: join([y[:, :192], gap, y[:, 192:256], gap, y[:, 256:]])
    couple_wide = lambda y: join([y[:, :128], gap, y[:, 128:192], gap, y[:, 192:]])
    solve_narrow = lambda y: join([y[:, :192], y[:, 256:320], y[:, 384:]])
    couple_narrow = lambda y: join([y[:, :128], y[:, 192:256], y[:, 320:]])
    solved[1] = core_summed_one(solve_narrow(dot(separator, solve[1])))
    part = total[0] - dot_t(couple_wide(solved[1].astype(BF16)), placed)
    separator = summed_over_chips(part, 4).astype(BF16)

    solved[0] = core_summed(dot(separator, solve[0]))

    solutions = []
    for level in range(4):
        residual = solved[level].astype(BF16)
        if level == 1:
            partial = core_summed_one(couple_narrow(dot(solutions[0], placed)))
            residual = (residual.astype(F32) - partial).astype(BF16)
            residual = solve_wide(residual)
        if level > 1:
            taken = sum(
                dot(solutions[above], is_at(targets[level], height[above], base(level, above), 0))
                for above in range(level)
            )
            partial = core_summed(dot(taken.astype(BF16), two_coupling if level == 2 else leaf_coupling))
            residual = (residual.astype(F32) - partial).astype(BF16)
        product = dot_t(residual, solve[level])
        if level < 3:
            product = summed_over_chips(product, 4 - level)
        solutions.append(product.astype(BF16))

    sending = [value.reshape(16, 16, -1).transpose(1, 0, 2) for value in solutions]
    returned = all_to_all(jnp.concatenate(sending, axis=2), "row")
    parts, at = [], 0
    for level in range(4):
        depth = sending[level].shape[2]
        part = returned[:, :, at : at + depth]
        at += depth
        if level < 3:
            planes = 32 // groups[level]
            part = lax.dynamic_slice_in_dim(part, chips[level] * planes, planes, 0)
            part = part.reshape(1, 2, planes * 8, depth)
            part = jnp.broadcast_to(part, (2, *part.shape[1:])).reshape(4, planes * 8, depth)
        else:
            part = part.reshape(4, 64, depth)
        parts.append(jnp.pad(part, ((0, 0), (0, 0), (0, LANES - depth))))
    shared = all_to_all(jnp.concatenate(parts, axis=1), "col", leaf_groups)
    near = lax.dynamic_slice_in_dim(shared, chips[3] * 2, 2, 0)
    results, at = [], 0
    for level in range(4):
        count, depth = parts[level].shape[1], sending[level].shape[2]
        if level < 3:
            part = near[:, at : at + count, :depth]
        else:
            both = shared[:, at : at + count, :depth].astype(F32).reshape(2, 2, count, depth)
            part = (both[0] + both[1]).astype(BF16)
        at += count
        results.append(jnp.concatenate([part[0], part[1]], axis=1).T)
    return tuple(results)


def solution(mesh):
    split = P("row", "col")
    in_specs = (P("col", "row"),) * 4 + (split,) * 7 + (P(),) * 3
    return jax.shard_map(
        per_device, mesh=mesh, in_specs=in_specs, out_specs=(split,) * 4, check_vma=False
    )
```

```python
import jax
import jax.numpy as jnp
from jax import lax
from jax.experimental.layout import Layout, with_layout_constraint
from jax.sharding import PartitionSpec as P

BF16 = jnp.bfloat16
F32 = jnp.float32
LANES = 128


def core_swapped(value):
    return lax.ppermute(value, "col", [(source, source ^ 1) for source in range(32)])


def all_to_all(value, axis, groups=None):
    return lax.all_to_all(
        value, axis, split_axis=0, concat_axis=0, tiled=True, axis_index_groups=groups
    )


def chip_groups(bits, stride=1):
    chips = 1 << bits
    return [
        [2 * (base + low + stride * chip) + core for chip in range(chips)]
        for base in range(0, 16, chips * stride)
        for low in range(stride)
        for core in range(2)
    ]


def summed_over_chips(value, bits):
    for part, stride in ((2, 1), (2, 4)) if bits == 4 else ((bits, 1),):
        chips = 1 << part
        copies = jnp.broadcast_to(value.astype(BF16)[None], (chips, *value.shape))
        got = all_to_all(copies, "col", chip_groups(part, stride))
        value = sum(got[chip].astype(F32) for chip in range(chips))
    return value


def after(value, earlier):
    return lax.optimization_barrier((value, earlier))[0]


def halves(block, core, axis=0):
    half = block.shape[axis] // 2
    return (
        lax.dynamic_slice_in_dim(block, core * half, half, axis),
        lax.dynamic_slice_in_dim(block, (1 - core) * half, half, axis),
    )


def dot(left, right):
    return lax.dot_general(left, right, (((1,), (0,)), ((), ())), preferred_element_type=F32)


def dot_t(left, right):
    return lax.dot_general(left, right, (((1,), (1,)), ((), ())), preferred_element_type=F32)


def core_summed(value):
    other = core_swapped(value)
    width = value.shape[1] // 2
    return value + jnp.concatenate([other[:, width:], other[:, :width]], axis=1)


def core_summed_one(value):
    other = core_swapped(value)
    return value + jnp.concatenate(
        [other[:, 256:], other[:, 192:256], other[:, 128:192], other[:, :128]], axis=1
    )


def is_at(target, rows, first, axis):
    shape = (rows, target.shape[0]) if axis == 0 else (target.shape[0], rows)
    spot = lax.broadcasted_iota(jnp.int32, shape, axis) + first
    return (spot == (target[None] if axis == 0 else target[:, None])).astype(BF16)


def looked_up(table, at):
    digits = jnp.stack([(table + 1) // 128, (table + 1) % 128]).astype(BF16)
    found = dot(digits, is_at(at, table.shape[0], 0, 0))
    return (found[0] * 128 + found[1]).astype(jnp.int32) - 1


def composite_targets(maps, fronts, orders, core):
    tables = [None] * 4
    for level in (1, 2, 3):
        parent = orders[level - 1]
        own = lax.dynamic_index_in_dim(maps[level - 1], fronts[level], 0, keepdims=False)
        block = parent // 16
        half = block // 2
        at = jnp.minimum(own, parent - 1)
        inside = at % block
        place = jnp.where(inside // half == core, at // block * half + inside % half, -1)
        if level > 1:
            further = looked_up(tables[level - 1], own - parent)
            further = jnp.where(further >= 0, further + parent // 2, -1)
            place = jnp.where(own < parent, place, further)
        tables[level] = place
    return tables


def per_device(
    inverse_top,
    inverse_one,
    inverse_two,
    inverse_leaf,
    coupling_one,
    coupling_two,
    coupling_leaf,
    rhs_top,
    rhs_one,
    rhs_two,
    rhs_leaf,
    parent_map_one,
    parent_map_two,
    parent_map_leaf,
):
    column = lax.axis_index("col")
    core = column % 2
    groups = [32, 16, 8, 4]
    orders = [4096, 3072, 2048, 1024]
    maps = [None, parent_map_one, parent_map_two, parent_map_leaf]
    fronts = [column // group for group in groups]
    chips = [column % group // 2 for group in groups]
    leaf_groups = [[4 * front + at for at in range(4)] for front in range(8)]
    join = lambda parts: jnp.concatenate(parts, axis=1)
    stack = lambda parts: jnp.concatenate(parts, axis=0)
    lanes = lambda block: [block[:, :LANES], block[:, LANES:]]

    spread = all_to_all(jnp.broadcast_to(rhs_leaf[None], (4, 64, 64)), "col", leaf_groups)

    def strips(one, two, coupled):
        tails = join([one[:, LANES:], coupled[:, LANES:]])
        return stack([one[:, :LANES]] + lanes(two) + [coupled[:, :LANES], tails])

    by_rows = lambda value: with_layout_constraint(value, Layout(major_to_minor=(0, 1)))
    blocks = [inverse_one.T, inverse_two.T, coupling_one]
    kept, sent = zip(*[halves(block, core) for block in blocks])
    taken = core_swapped(by_rows(strips(*sent)))
    packed = stack([strips(*kept)] + lanes(coupling_two) + [taken])
    middle = lax.all_gather(by_rows(packed), "row", axis=0)

    leaf_columns = spread.transpose(0, 2, 1).reshape(256, 64)
    leaf_products = dot_t(leaf_columns, inverse_leaf).astype(BF16)

    sides = [side.T for side in (rhs_top, rhs_one, rhs_two)]
    side_kept, side_sent = zip(*[halves(side, core, 1) for side in sides])
    pad = lambda part: jnp.pad(part, ((0, 0), (0, LANES - part.shape[1])))
    side_taken = core_swapped(stack([pad(part) for part in side_sent]))
    outgoing, at = [leaf_products.reshape(16, 16, 256)], 0
    for level in range(3):
        mine = side_kept[level]
        count, depth = mine.shape
        other = side_taken[at : at + count, :depth]
        at += count
        both = jnp.where(core == 0, stack([mine, other]), stack([other, mine]))
        planes = 2 * count // 16
        outgoing.append(
            lax.dynamic_update_slice(
                jnp.zeros((16, 16, depth), BF16),
                both.reshape(planes, 16, depth),
                (chips[level] * planes, 0, 0),
            )
        )
    sending = jnp.concatenate(outgoing, axis=2)
    incoming = all_to_all(sending, "row")
    leaf_own = jnp.sum(incoming[:, :, :256].astype(F32), axis=0).astype(BF16)
    total, at = [], 256
    for level in range(3):
        depth = side_kept[level].shape[1]
        part = incoming[:, :, at : at + depth].transpose(1, 0, 2)
        total.append(part.reshape(16, 16 * depth).astype(F32))
        at += depth

    blocks = [block.T for block in after((inverse_top, inverse_leaf), sending)]
    kept, sent = zip(*[halves(block, core) for block in blocks])
    ends = lambda top, leaf: stack([top] + lanes(leaf))
    packed = by_rows(stack([ends(*kept), core_swapped(by_rows(ends(*sent)))]))

    leaf_rows = lax.all_gather(after(coupling_leaf, sending), "row", axis=0, tiled=True)
    update = dot_t(leaf_own, leaf_rows)
    update = (update + core_swapped(update)).astype(BF16)

    targets = composite_targets(after(maps[1:], sending), fronts, orders, core)
    height = [order // 2 for order in orders]
    base = lambda level, above: sum(height[above + 1 : level])

    def leaf_share(above):
        return dot(update, is_at(targets[3], height[above], base(3, above), 1))

    separator = summed_over_chips(total[2] - leaf_share(2), 2).astype(BF16)
    total[1] = total[1] - leaf_share(1)
    total[0] = total[0] - leaf_share(0)

    leaf_coupling = join([leaf_rows, core_swapped(after(leaf_rows, update))])
    leaf_solved = join([leaf_own, core_swapped(after(leaf_own, update))])
    separator, leaf_coupling, leaf_solved, packed, *total[:2] = lax.optimization_barrier(
        (separator, leaf_coupling, leaf_solved, packed, *total[:2])
    )
    outer = lax.all_gather(packed, "row", axis=0)

    solve, solved = [None] * 4, [None, None, None, leaf_solved]
    rows_of = lambda value, at, depth: value[:, at : at + depth].reshape(16 * depth, LANES)

    def share(update, level, above, target):
        return dot(update, is_at(target, height[above], base(level, above), 1))

    far = 416 + 256
    solve[2] = join([rows_of(middle, at, 64) for at in (96, 160, far + 96, far + 160)])
    two_rows = join([rows_of(middle, 416, 128), rows_of(middle, 544, 128)])
    two_coupling = join([two_rows, core_swapped(two_rows)])
    solved[2] = core_summed(dot(separator, solve[2]))
    update_two = dot_t(solved[2].astype(BF16), two_coupling).astype(BF16)
    part = total[1] - share(update_two, 2, 1, targets[2])
    separator = summed_over_chips(part, 3).astype(BF16)

    late, late_two = after((middle, targets[2]), part)
    main, tail, far_tail = rows_of(late, 224, 96), rows_of(late, 320, 96), rows_of(late, far + 320, 96)
    solve[1] = join([rows_of(late, 0, 96), tail, far_tail, rows_of(late, far, 96)])
    coupling = join([main, tail, far_tail, rows_of(late, far + 224, 96)])
    swapped = core_swapped(coupling)
    other = join([swapped[:, at : at + LANES] for at in (384, 256, 128, 0)])
    cut = targets[1].reshape(16, 2, 96)
    here = jnp.where(core == 0, cut[:, 0], cut[:, 1]).reshape(1536)
    there = jnp.where(core == 0, cut[:, 1], cut[:, 0]).reshape(1536)
    here, there = after((here, there), part)
    total[0] = total[0] - share(update_two, 2, 0, late_two)
    placed = dot(is_at(here, height[0], 0, 0), coupling).astype(BF16)
    separator, total[0], placed = lax.optimization_barrier((separator, total[0], placed))
    placed = (placed.astype(F32) + dot(is_at(there, height[0], 0, 0), other)).astype(BF16)
    placed = lax.optimization_barrier(placed)
    gap = jnp.zeros((16, 64), BF16)
    solve_wide = lambda y: join([y[:, :192], gap, y[:, 192:256], gap, y[:, 256:]])
    couple_wide = lambda y: join([y[:, :128], gap, y[:, 128:192], gap, y[:, 192:]])
    solve_narrow = lambda y: join([y[:, :192], y[:, 256:320], y[:, 384:]])
    couple_narrow = lambda y: join([y[:, :128], y[:, 192:256], y[:, 320:]])
    solved[1] = core_summed_one(solve_narrow(dot(separator, solve[1])))
    part = total[0] - dot_t(couple_wide(solved[1].astype(BF16)), placed)
    separator = summed_over_chips(part, 4).astype(BF16)


    outer = after(outer, separator)
    solve[0] = join([rows_of(outer, 0, 128), rows_of(outer, 192, 128)])
    solve[3] = join([rows_of(outer, at, 32) for at in (128, 160, 320, 352)])
    solved[0] = core_summed(dot(separator, solve[0]))

    solutions = []
    for level in range(4):
        residual = solved[level].astype(BF16)
        if level == 1:
            partial = core_summed_one(couple_narrow(dot(solutions[0], placed)))
            residual = (residual.astype(F32) - partial).astype(BF16)
            residual = solve_wide(residual)
        if level > 1:
            taken = sum(
                dot(solutions[above], is_at(targets[level], height[above], base(level, above), 0))
                for above in range(level)
            )
            partial = core_summed(dot(taken.astype(BF16), two_coupling if level == 2 else leaf_coupling))
            residual = (residual.astype(F32) - partial).astype(BF16)
        product = dot_t(residual, solve[level])
        if level < 3:
            product = summed_over_chips(product, 4 - level)
        solutions.append(product.astype(BF16))

    sending = [value.reshape(16, 16, -1).transpose(1, 0, 2) for value in solutions]
    returned = all_to_all(jnp.concatenate(sending, axis=2), "row")
    parts, at = [], 0
    for level in range(4):
        depth = sending[level].shape[2]
        part = returned[:, :, at : at + depth]
        at += depth
        if level < 3:
            planes = 32 // groups[level]
            part = lax.dynamic_slice_in_dim(part, chips[level] * planes, planes, 0)
            part = part.reshape(1, 2, planes * 8, depth)
            part = jnp.broadcast_to(part, (2, *part.shape[1:])).reshape(4, planes * 8, depth)
        else:
            part = part.reshape(4, 64, depth)
        parts.append(jnp.pad(part, ((0, 0), (0, 0), (0, LANES - depth))))
    shared = all_to_all(jnp.concatenate(parts, axis=1), "col", leaf_groups)
    near = lax.dynamic_slice_in_dim(shared, chips[3] * 2, 2, 0)
    results, at = [], 0
    for level in range(4):
        count, depth = parts[level].shape[1], sending[level].shape[2]
        if level < 3:
            part = near[:, at : at + count, :depth]
        else:
            both = shared[:, at : at + count, :depth].astype(F32).reshape(2, 2, count, depth)
            part = (both[0] + both[1]).astype(BF16)
        at += count
        results.append(jnp.concatenate([part[0], part[1]], axis=1).T)
    return tuple(results)


def solution(mesh):
    split = P("row", "col")
    in_specs = (P("col", "row"),) * 4 + (split,) * 7 + (P(),) * 3
    return jax.shard_map(
        per_device, mesh=mesh, in_specs=in_specs, out_specs=(split,) * 4, check_vma=False
    )
```

```python
import jax
import jax.numpy as jnp
from jax import lax
from jax.experimental.layout import Layout, with_layout_constraint
from jax.sharding import PartitionSpec as P

BF16 = jnp.bfloat16
F32 = jnp.float32
LANES = 128


def core_swapped(value):
    return lax.ppermute(value, "col", [(source, source ^ 1) for source in range(32)])


def all_to_all(value, axis, groups=None):
    return lax.all_to_all(
        value, axis, split_axis=0, concat_axis=0, tiled=True, axis_index_groups=groups
    )


def chip_groups(bits, stride=1):
    chips = 1 << bits
    return [
        [2 * (base + low + stride * chip) + core for chip in range(chips)]
        for base in range(0, 16, chips * stride)
        for low in range(stride)
        for core in range(2)
    ]


def summed_over_chips(value, bits):
    for part, stride in ((2, 1), (2, 4)) if bits == 4 else ((bits, 1),):
        chips = 1 << part
        copies = jnp.broadcast_to(value.astype(BF16)[None], (chips, *value.shape))
        got = all_to_all(copies, "col", chip_groups(part, stride))
        value = sum(got[chip].astype(F32) for chip in range(chips))
    return value


def after(value, earlier):
    return lax.optimization_barrier((value, earlier))[0]


def halves(block, core, axis=0):
    half = block.shape[axis] // 2
    return (
        lax.dynamic_slice_in_dim(block, core * half, half, axis),
        lax.dynamic_slice_in_dim(block, (1 - core) * half, half, axis),
    )


def dot(left, right):
    return lax.dot_general(left, right, (((1,), (0,)), ((), ())), preferred_element_type=F32)


def dot_t(left, right):
    return lax.dot_general(left, right, (((1,), (1,)), ((), ())), preferred_element_type=F32)


def core_summed(value):
    other = core_swapped(value)
    width = value.shape[1] // 2
    return value + jnp.concatenate([other[:, width:], other[:, :width]], axis=1)


def core_summed_one(value):
    other = core_swapped(value)
    return value + jnp.concatenate(
        [other[:, 256:], other[:, 192:256], other[:, 128:192], other[:, :128]], axis=1
    )


def is_at(target, rows, first, axis):
    shape = (rows, target.shape[0]) if axis == 0 else (target.shape[0], rows)
    spot = lax.broadcasted_iota(jnp.int32, shape, axis) + first
    return (spot == (target[None] if axis == 0 else target[:, None])).astype(BF16)


def looked_up(table, at):
    digits = jnp.stack([(table + 1) // 128, (table + 1) % 128]).astype(BF16)
    found = dot(digits, is_at(at, table.shape[0], 0, 0))
    return (found[0] * 128 + found[1]).astype(jnp.int32) - 1


def composite_targets(maps, fronts, orders, core):
    tables = [None] * 4
    for level in (1, 2, 3):
        parent = orders[level - 1]
        own = lax.dynamic_index_in_dim(maps[level - 1], fronts[level], 0, keepdims=False)
        block = parent // 16
        half = block // 2
        at = jnp.minimum(own, parent - 1)
        inside = at % block
        place = jnp.where(inside // half == core, at // block * half + inside % half, -1)
        if level > 1:
            further = looked_up(tables[level - 1], own - parent)
            further = jnp.where(further >= 0, further + parent // 2, -1)
            place = jnp.where(own < parent, place, further)
        tables[level] = place
    return tables


def per_device(
    inverse_top,
    inverse_one,
    inverse_two,
    inverse_leaf,
    coupling_one,
    coupling_two,
    coupling_leaf,
    rhs_top,
    rhs_one,
    rhs_two,
    rhs_leaf,
    parent_map_one,
    parent_map_two,
    parent_map_leaf,
):
    column = lax.axis_index("col")
    core = column % 2
    groups = [32, 16, 8, 4]
    orders = [4096, 3072, 2048, 1024]
    maps = [None, parent_map_one, parent_map_two, parent_map_leaf]
    fronts = [column // group for group in groups]
    chips = [column % group // 2 for group in groups]
    leaf_groups = [[4 * front + at for at in range(4)] for front in range(8)]
    join = lambda parts: jnp.concatenate(parts, axis=1)
    stack = lambda parts: jnp.concatenate(parts, axis=0)
    lanes = lambda block: [block[:, :LANES], block[:, LANES:]]

    spread = all_to_all(jnp.broadcast_to(rhs_leaf[None], (4, 64, 64)), "col", leaf_groups)

    def strips(one, two, top, leaf, coupled):
        tails = join([one[:, LANES:], coupled[:, LANES:]])
        parts = [one[:, :LANES]] + lanes(two) + [top] + lanes(leaf)
        return stack(parts + [coupled[:, :LANES], tails])

    by_rows = lambda value: with_layout_constraint(value, Layout(major_to_minor=(0, 1)))
    blocks = [inverse_one.T, inverse_two.T, inverse_top.T, inverse_leaf.T, coupling_one]
    kept, sent = zip(*[halves(block, core) for block in blocks])
    taken = core_swapped(by_rows(strips(*sent)))
    packed = stack([strips(*kept)] + lanes(coupling_two) + [taken])
    upper = lax.all_gather(by_rows(packed), "row", axis=0)

    leaf_columns = spread.transpose(0, 2, 1).reshape(256, 64)
    leaf_products = dot_t(leaf_columns, inverse_leaf).astype(BF16)

    sides = [side.T for side in (rhs_top, rhs_one, rhs_two)]
    side_kept, side_sent = zip(*[halves(side, core, 1) for side in sides])
    pad = lambda part: jnp.pad(part, ((0, 0), (0, LANES - part.shape[1])))
    side_taken = core_swapped(stack([pad(part) for part in side_sent]))
    outgoing, at = [leaf_products.reshape(16, 16, 256)], 0
    for level in range(3):
        mine = side_kept[level]
        count, depth = mine.shape
        other = side_taken[at : at + count, :depth]
        at += count
        both = jnp.where(core == 0, stack([mine, other]), stack([other, mine]))
        planes = 2 * count // 16
        outgoing.append(
            lax.dynamic_update_slice(
                jnp.zeros((16, 16, depth), BF16),
                both.reshape(planes, 16, depth),
                (chips[level] * planes, 0, 0),
            )
        )
    sending = jnp.concatenate(outgoing, axis=2)
    incoming = all_to_all(sending, "row")
    leaf_own = jnp.sum(incoming[:, :, :256].astype(F32), axis=0).astype(BF16)
    total, at = [], 256
    for level in range(3):
        depth = side_kept[level].shape[1]
        part = incoming[:, :, at : at + depth].transpose(1, 0, 2)
        total.append(part.reshape(16, 16 * depth).astype(F32))
        at += depth

    leaf_rows = lax.all_gather(after(coupling_leaf, sending), "row", axis=0, tiled=True)
    update = dot_t(leaf_own, leaf_rows)
    update = (update + core_swapped(update)).astype(BF16)

    targets = composite_targets(after(maps[1:], sending), fronts, orders, core)
    height = [order // 2 for order in orders]
    base = lambda level, above: sum(height[above + 1 : level])

    def leaf_share(above):
        return dot(update, is_at(targets[3], height[above], base(3, above), 1))

    separator = summed_over_chips(total[2] - leaf_share(2), 2).astype(BF16)
    total[1] = total[1] - leaf_share(1)
    total[0] = total[0] - leaf_share(0)

    leaf_coupling = join([leaf_rows, core_swapped(after(leaf_rows, update))])
    leaf_solved = join([leaf_own, core_swapped(after(leaf_own, update))])
    separator, leaf_coupling, leaf_solved, *total[:2] = lax.optimization_barrier(
        (separator, leaf_coupling, leaf_solved, *total[:2])
    )

    solve, solved = [None] * 4, [None, None, None, leaf_solved]
    rows_of = lambda value, at, depth: value[:, at : at + depth].reshape(16 * depth, LANES)

    def share(update, level, above, target):
        return dot(update, is_at(target, height[above], base(level, above), 1))

    far = 608 + 256
    solve[2] = join([rows_of(upper, at, 64) for at in (96, 160, far + 96, far + 160)])
    two_rows = join([rows_of(upper, 608, 128), rows_of(upper, 736, 128)])
    two_coupling = join([two_rows, core_swapped(two_rows)])
    solved[2] = core_summed(dot(separator, solve[2]))
    update_two = dot_t(solved[2].astype(BF16), two_coupling).astype(BF16)
    part = total[1] - share(update_two, 2, 1, targets[2])
    separator = summed_over_chips(part, 3).astype(BF16)

    late, late_two = after((upper, targets[2]), part)
    main, tail, far_tail = rows_of(late, 416, 96), rows_of(late, 512, 96), rows_of(late, far + 512, 96)
    solve[1] = join([rows_of(late, 0, 96), tail, far_tail, rows_of(late, far, 96)])
    coupling = join([main, tail, far_tail, rows_of(late, far + 416, 96)])
    swapped = core_swapped(coupling)
    other = join([swapped[:, at : at + LANES] for at in (384, 256, 128, 0)])
    cut = targets[1].reshape(16, 2, 96)
    here = jnp.where(core == 0, cut[:, 0], cut[:, 1]).reshape(1536)
    there = jnp.where(core == 0, cut[:, 1], cut[:, 0]).reshape(1536)
    here, there = after((here, there), part)
    total[0] = total[0] - share(update_two, 2, 0, late_two)
    placed = dot(is_at(here, height[0], 0, 0), coupling).astype(BF16)
    separator, total[0], placed = lax.optimization_barrier((separator, total[0], placed))
    placed = (placed.astype(F32) + dot(is_at(there, height[0], 0, 0), other)).astype(BF16)
    placed = lax.optimization_barrier(placed)
    gap = jnp.zeros((16, 64), BF16)
    solve_wide = lambda y: join([y[:, :192], gap, y[:, 192:256], gap, y[:, 256:]])
    couple_wide = lambda y: join([y[:, :128], gap, y[:, 128:192], gap, y[:, 192:]])
    solve_narrow = lambda y: join([y[:, :192], y[:, 256:320], y[:, 384:]])
    couple_narrow = lambda y: join([y[:, :128], y[:, 192:256], y[:, 320:]])
    solved[1] = core_summed_one(solve_narrow(dot(separator, solve[1])))
    part = total[0] - dot_t(couple_wide(solved[1].astype(BF16)), placed)
    separator = summed_over_chips(part, 4).astype(BF16)


    late = after(upper, separator)
    solve[0] = join([rows_of(late, 224, 128), rows_of(late, far + 224, 128)])
    solve[3] = join([rows_of(late, at, 32) for at in (352, 384, far + 352, far + 384)])
    solved[0] = core_summed(dot(separator, solve[0]))

    solutions = []
    for level in range(4):
        residual = solved[level].astype(BF16)
        if level == 1:
            partial = core_summed_one(couple_narrow(dot(solutions[0], placed)))
            residual = (residual.astype(F32) - partial).astype(BF16)
            residual = solve_wide(residual)
        if level > 1:
            taken = sum(
                dot(solutions[above], is_at(targets[level], height[above], base(level, above), 0))
                for above in range(level)
            )
            partial = core_summed(dot(taken.astype(BF16), two_coupling if level == 2 else leaf_coupling))
            residual = (residual.astype(F32) - partial).astype(BF16)
        product = dot_t(residual, solve[level])
        if level < 3:
            product = summed_over_chips(product, 4 - level)
        solutions.append(product.astype(BF16))

    sending = [value.reshape(16, 16, -1).transpose(1, 0, 2) for value in solutions]
    returned = all_to_all(jnp.concatenate(sending, axis=2), "row")
    parts, at = [], 0
    for level in range(4):
        depth = sending[level].shape[2]
        part = returned[:, :, at : at + depth]
        at += depth
        if level < 3:
            planes = 32 // groups[level]
            part = lax.dynamic_slice_in_dim(part, chips[level] * planes, planes, 0)
            part = part.reshape(1, 2, planes * 8, depth)
            part = jnp.broadcast_to(part, (2, *part.shape[1:])).reshape(4, planes * 8, depth)
        else:
            part = part.reshape(4, 64, depth)
        parts.append(jnp.pad(part, ((0, 0), (0, 0), (0, LANES - depth))))
    shared = all_to_all(jnp.concatenate(parts, axis=1), "col", leaf_groups)
    near = lax.dynamic_slice_in_dim(shared, chips[3] * 2, 2, 0)
    results, at = [], 0
    for level in range(4):
        count, depth = parts[level].shape[1], sending[level].shape[2]
        if level < 3:
            part = near[:, at : at + count, :depth]
        else:
            both = shared[:, at : at + count, :depth].astype(F32).reshape(2, 2, count, depth)
            part = (both[0] + both[1]).astype(BF16)
        at += count
        results.append(jnp.concatenate([part[0], part[1]], axis=1).T)
    return tuple(results)


def solution(mesh):
    split = P("row", "col")
    in_specs = (P("col", "row"),) * 4 + (split,) * 7 + (P(),) * 3
    return jax.shard_map(
        per_device, mesh=mesh, in_specs=in_specs, out_specs=(split,) * 4, check_vma=False
    )
```

```python
import jax
import jax.numpy as jnp
from jax import lax
from jax.experimental.layout import Layout, with_layout_constraint
from jax.sharding import PartitionSpec as P

BF16 = jnp.bfloat16
F32 = jnp.float32
LANES = 128


def core_swapped(value):
    return lax.ppermute(value, "col", [(source, source ^ 1) for source in range(32)])


def all_to_all(value, axis, groups=None):
    return lax.all_to_all(
        value, axis, split_axis=0, concat_axis=0, tiled=True, axis_index_groups=groups
    )


def chip_groups(bits, stride=1):
    chips = 1 << bits
    return [
        [2 * (base + low + stride * chip) + core for chip in range(chips)]
        for base in range(0, 16, chips * stride)
        for low in range(stride)
        for core in range(2)
    ]


def summed_over_chips(value, bits):
    for part, stride in ((2, 1), (2, 4)) if bits == 4 else ((bits, 1),):
        chips = 1 << part
        copies = jnp.broadcast_to(value.astype(BF16)[None], (chips, *value.shape))
        got = all_to_all(copies, "col", chip_groups(part, stride))
        value = sum(got[chip].astype(F32) for chip in range(chips))
    return value


def after(value, earlier):
    return lax.optimization_barrier((value, earlier))[0]


def halves(block, core, axis=0):
    half = block.shape[axis] // 2
    return (
        lax.dynamic_slice_in_dim(block, core * half, half, axis),
        lax.dynamic_slice_in_dim(block, (1 - core) * half, half, axis),
    )


def dot(left, right):
    return lax.dot_general(left, right, (((1,), (0,)), ((), ())), preferred_element_type=F32)


def dot_t(left, right):
    return lax.dot_general(left, right, (((1,), (1,)), ((), ())), preferred_element_type=F32)


def core_summed(value):
    other = core_swapped(value)
    width = value.shape[1] // 2
    return value + jnp.concatenate([other[:, width:], other[:, :width]], axis=1)


def core_summed_one(value):
    other = core_swapped(value)
    return value + jnp.concatenate(
        [other[:, 256:], other[:, 192:256], other[:, 128:192], other[:, :128]], axis=1
    )


def is_at(target, rows, first, axis):
    shape = (rows, target.shape[0]) if axis == 0 else (target.shape[0], rows)
    spot = lax.broadcasted_iota(jnp.int32, shape, axis) + first
    return (spot == (target[None] if axis == 0 else target[:, None])).astype(BF16)


def looked_up(table, at):
    digits = jnp.stack([(table + 1) // 128, (table + 1) % 128]).astype(BF16)
    found = dot(digits, is_at(at, table.shape[0], 0, 0))
    return (found[0] * 128 + found[1]).astype(jnp.int32) - 1


def composite_targets(maps, fronts, orders, core):
    tables = [None] * 4
    for level in (1, 2, 3):
        parent = orders[level - 1]
        own = lax.dynamic_index_in_dim(maps[level - 1], fronts[level], 0, keepdims=False)
        block = parent // 16
        half = block // 2
        at = jnp.minimum(own, parent - 1)
        inside = at % block
        place = jnp.where(inside // half == core, at // block * half + inside % half, -1)
        if level > 1:
            further = looked_up(tables[level - 1], own - parent)
            further = jnp.where(further >= 0, further + parent // 2, -1)
            place = jnp.where(own < parent, place, further)
        tables[level] = place
    return tables


def per_device(
    inverse_top,
    inverse_one,
    inverse_two,
    inverse_leaf,
    coupling_one,
    coupling_two,
    coupling_leaf,
    rhs_top,
    rhs_one,
    rhs_two,
    rhs_leaf,
    parent_map_one,
    parent_map_two,
    parent_map_leaf,
):
    column = lax.axis_index("col")
    core = column % 2
    groups = [32, 16, 8, 4]
    orders = [4096, 3072, 2048, 1024]
    maps = [None, parent_map_one, parent_map_two, parent_map_leaf]
    fronts = [column // group for group in groups]
    chips = [column % group // 2 for group in groups]
    leaf_groups = [[4 * front + at for at in range(4)] for front in range(8)]
    join = lambda parts: jnp.concatenate(parts, axis=1)
    stack = lambda parts: jnp.concatenate(parts, axis=0)
    lanes = lambda block: [block[:, :LANES], block[:, LANES:]]

    spread = all_to_all(jnp.broadcast_to(rhs_leaf[None], (4, 64, 64)), "col", leaf_groups)

    def strips(one, two, top, leaf, coupled):
        tails = join([one[:, LANES:], coupled[:, LANES:]])
        parts = [one[:, :LANES]] + lanes(two) + [top] + lanes(leaf)
        return stack(parts + [coupled[:, :LANES], tails])

    by_rows = lambda value: with_layout_constraint(value, Layout(major_to_minor=(0, 1)))
    blocks = [inverse_one.T, inverse_two.T, inverse_top.T, inverse_leaf.T, coupling_one]
    kept, sent = zip(*[halves(block, core) for block in blocks])
    taken = core_swapped(by_rows(strips(*sent)))
    packed = stack([strips(*kept)] + lanes(coupling_two) + [taken])
    upper = lax.all_gather(by_rows(packed), "row", axis=0)

    leaf_columns = spread.transpose(0, 2, 1).reshape(256, 64)
    leaf_products = dot_t(leaf_columns, inverse_leaf).astype(BF16)

    sides = [side.T for side in (rhs_top, rhs_one, rhs_two)]
    side_kept, side_sent = zip(*[halves(side, core, 1) for side in sides])
    pad = lambda part: jnp.pad(part, ((0, 0), (0, LANES - part.shape[1])))
    side_taken = core_swapped(stack([pad(part) for part in side_sent]))
    outgoing, at = [leaf_products.reshape(16, 16, 256)], 0
    for level in range(3):
        mine = side_kept[level]
        count, depth = mine.shape
        other = side_taken[at : at + count, :depth]
        at += count
        both = jnp.where(core == 0, stack([mine, other]), stack([other, mine]))
        planes = 2 * count // 16
        outgoing.append(
            lax.dynamic_update_slice(
                jnp.zeros((16, 16, depth), BF16),
                both.reshape(planes, 16, depth),
                (chips[level] * planes, 0, 0),
            )
        )
    sending = jnp.concatenate(outgoing, axis=2)
    incoming = all_to_all(sending, "row")
    leaf_own = jnp.sum(incoming[:, :, :256].astype(F32), axis=0).astype(BF16)
    total, at = [], 256
    for level in range(3):
        depth = side_kept[level].shape[1]
        part = incoming[:, :, at : at + depth].transpose(1, 0, 2)
        total.append(part.reshape(16, 16 * depth).astype(F32))
        at += depth

    leaf_rows = lax.all_gather(after(coupling_leaf, sending), "row", axis=0, tiled=True)
    update = dot_t(leaf_own, leaf_rows)
    update = (update + core_swapped(update)).astype(BF16)

    targets = composite_targets(after(maps[1:], sending), fronts, orders, core)
    height = [order // 2 for order in orders]
    base = lambda level, above: sum(height[above + 1 : level])

    def leaf_share(above):
        return dot(update, is_at(targets[3], height[above], base(3, above), 1))

    separator = summed_over_chips(total[2] - leaf_share(2), 2).astype(BF16)
    total[1] = total[1] - leaf_share(1)
    total[0] = total[0] - leaf_share(0)

    leaf_coupling = join([leaf_rows, core_swapped(after(leaf_rows, update))])
    leaf_solved = join([leaf_own, core_swapped(after(leaf_own, update))])
    separator, leaf_coupling, leaf_solved, *total[:2] = lax.optimization_barrier(
        (separator, leaf_coupling, leaf_solved, *total[:2])
    )

    solve, solved = [None] * 4, [None, None, None, leaf_solved]
    rows_of = lambda value, at, depth: value[:, at : at + depth].reshape(16 * depth, LANES)

    def share(update, level, above, target):
        return dot(update, is_at(target, height[above], base(level, above), 1))

    far = 608 + 256
    solve[2] = join([rows_of(upper, at, 64) for at in (96, 160, far + 96, far + 160)])
    two_rows = join([rows_of(upper, 608, 128), rows_of(upper, 736, 128)])
    two_coupling = join([two_rows, core_swapped(two_rows)])
    solved[2] = core_summed(dot(separator, solve[2]))
    update_two = dot_t(solved[2].astype(BF16), two_coupling).astype(BF16)
    part = total[1] - share(update_two, 2, 1, targets[2])
    separator = summed_over_chips(part, 3).astype(BF16)

    late, late_two = after((upper, targets[2]), part)
    main, tail, far_tail = rows_of(late, 416, 96), rows_of(late, 512, 96), rows_of(late, far + 512, 96)
    solve[1] = join([rows_of(late, 0, 96), tail, far_tail, rows_of(late, far, 96)])
    far_main = rows_of(late, far + 416, 96)
    coupling = join([main, tail, far_tail, far_main])
    other = core_swapped(join([far_main, far_tail, tail, main]))
    cut = targets[1].reshape(16, 2, 96)
    here = jnp.where(core == 0, cut[:, 0], cut[:, 1]).reshape(1536)
    there = jnp.where(core == 0, cut[:, 1], cut[:, 0]).reshape(1536)
    here, there = after((here, there), part)
    total[0] = total[0] - share(update_two, 2, 0, late_two)
    placed = dot(is_at(here, height[0], 0, 0), coupling).astype(BF16)
    separator, total[0], placed = lax.optimization_barrier((separator, total[0], placed))
    placed = (placed.astype(F32) + dot(is_at(there, height[0], 0, 0), other)).astype(BF16)
    placed = lax.optimization_barrier(placed)
    gap = jnp.zeros((16, 64), BF16)
    solve_wide = lambda y: join([y[:, :192], gap, y[:, 192:256], gap, y[:, 256:]])
    couple_wide = lambda y: join([y[:, :128], gap, y[:, 128:192], gap, y[:, 192:]])
    solve_narrow = lambda y: join([y[:, :192], y[:, 256:320], y[:, 384:]])
    couple_narrow = lambda y: join([y[:, :128], y[:, 192:256], y[:, 320:]])
    solved[1] = core_summed_one(solve_narrow(dot(separator, solve[1])))
    part = total[0] - dot_t(couple_wide(solved[1].astype(BF16)), placed)
    separator = summed_over_chips(part, 4).astype(BF16)


    late = after(upper, separator)
    solve[0] = join([rows_of(late, 224, 128), rows_of(late, far + 224, 128)])
    solve[3] = join([rows_of(late, at, 32) for at in (352, 384, far + 352, far + 384)])
    solved[0] = core_summed(dot(separator, solve[0]))

    solutions = []
    for level in range(4):
        residual = solved[level].astype(BF16)
        if level == 1:
            partial = core_summed_one(couple_narrow(dot(solutions[0], placed)))
            residual = (residual.astype(F32) - partial).astype(BF16)
            residual = solve_wide(residual)
        if level > 1:
            taken = sum(
                dot(solutions[above], is_at(targets[level], height[above], base(level, above), 0))
                for above in range(level)
            )
            partial = core_summed(dot(taken.astype(BF16), two_coupling if level == 2 else leaf_coupling))
            residual = (residual.astype(F32) - partial).astype(BF16)
        product = dot_t(residual, solve[level])
        if level < 3:
            product = summed_over_chips(product, 4 - level)
        solutions.append(product.astype(BF16))

    sending = [value.reshape(16, 16, -1).transpose(1, 0, 2) for value in solutions]
    returned = all_to_all(jnp.concatenate(sending, axis=2), "row")
    parts, at = [], 0
    for level in range(4):
        depth = sending[level].shape[2]
        part = returned[:, :, at : at + depth]
        at += depth
        if level < 3:
            planes = 32 // groups[level]
            part = lax.dynamic_slice_in_dim(part, chips[level] * planes, planes, 0)
            part = part.reshape(1, 2, planes * 8, depth)
            part = jnp.broadcast_to(part, (2, *part.shape[1:])).reshape(4, planes * 8, depth)
        else:
            part = part.reshape(4, 64, depth)
        parts.append(jnp.pad(part, ((0, 0), (0, 0), (0, LANES - depth))))
    shared = all_to_all(jnp.concatenate(parts, axis=1), "col", leaf_groups)
    near = lax.dynamic_slice_in_dim(shared, chips[3] * 2, 2, 0)
    results, at = [], 0
    for level in range(4):
        count, depth = parts[level].shape[1], sending[level].shape[2]
        if level < 3:
            part = near[:, at : at + count, :depth]
        else:
            both = shared[:, at : at + count, :depth].astype(F32).reshape(2, 2, count, depth)
            part = (both[0] + both[1]).astype(BF16)
        at += count
        results.append(jnp.concatenate([part[0], part[1]], axis=1).T)
    return tuple(results)


def solution(mesh):
    split = P("row", "col")
    in_specs = (P("col", "row"),) * 4 + (split,) * 7 + (P(),) * 3
    return jax.shard_map(
        per_device, mesh=mesh, in_specs=in_specs, out_specs=(split,) * 4, check_vma=False
    )
```
